32 devices in a mesh: gx: 8 (over z, x), gy: 4 (over y, core).
Axes of the slice: x: 2, y: 2, z: 4, core: 2. Of those that a mesh axis runs over, the one named last changes fastest.
Arguments:
- krylov_block: float32 [16, 26, 64, 1024], P(None, None, 'gx', 'gy'), may hold values from -13 to 13
- prior_basis: float32 [24, 26, 64, 1024], P(None, None, 'gx', 'gy'), may hold values from -5.2 to 5.2
- flux_along: float32 [26, 26], replicated, may hold values from -1.25 to 1.25
- flux_across: float32 [26, 26], replicated, may hold values from -1.25 to 1.25
- collision: float32 [64, 1024], P('gx', 'gy'), may hold values from 1 to 10
- field_rates: float32 [26], replicated, may hold values from 0.5 to 2
- wall_table: float32 [4, 26], replicated, may hold values from 0.5 to 3
- wall_mask: int32 [64, 1024], P('gx', 'gy'), may hold values 0 or 1
- wall_type: int32 [64, 1024], P('gx', 'gy'), may hold values from 0 to 3
Outputs:
- new_block: float32 [16, 26, 64, 1024], P(None, None, 'gx', 'gy')
- projection: float32 [24, 16], replicated
- triangle: float32 [16, 16], replicated
The draws below stay inside these ranges and needn't reach their ends.
All inputs are finite; a program needn't handle non-finite values. No bound on the sum of `wall_mask` on one device may be relied on, other than what follows from the above.
Results may differ from the reference program's by a relative error of at most 0.0003.
Values sent between devices are 32-bit elements; how exact they have to be, the bound alone decides.
A program may use at most 128 MiB of HBM per device.

```python
import math
import jax
import jax.numpy as jnp
from jax import lax

FIELDS = 26
BLOCK = 16
PRIOR = 24
TYPES = 4
NX = 64
NY = 1024


def rough_field(key, extent):
    return jax.random.truncated_normal(key, -4.0, 4.0, extent, jnp.float32)


def common_parts(key):
    folded = jax.random.fold_in(key, 7101)
    common = rough_field(jax.random.fold_in(folded, 1), (FIELDS, NX, NY))
    detail = rough_field(jax.random.fold_in(folded, 3), (BLOCK, FIELDS, NX, NY))
    return (common, detail)


def stratified(key, number, lowest):
    ranking = jax.random.permutation(jax.random.fold_in(key, 1), number).astype(jnp.float32)
    jitter = jax.random.uniform(jax.random.fold_in(key, 2), (number,), jnp.float32)
    return lowest * jnp.power(10.0, (ranking + jitter) / number)


def draw_krylov_block(key, part):
    common, detail = common_parts(key)
    column_scale = stratified(jax.random.fold_in(key, 7201), BLOCK, 0.3)
    mixing = stratified(jax.random.fold_in(key, 7202), BLOCK, 0.008)
    return column_scale[:, None, None, None] * (common[None] + mixing[:, None, None, None] * detail)


def draw_prior_basis(key, part):
    common, detail = common_parts(key)
    own_part = rough_field(jax.random.fold_in(key, 7301), (PRIOR, FIELDS, NX, NY))
    tilt_weight = jax.random.uniform(jax.random.fold_in(key, 7302), (PRIOR,), jnp.float32, -0.1, 0.1)
    linked = detail[jnp.arange(PRIOR) % BLOCK]
    scale_back = 1.0 / jnp.sqrt(1.0 + tilt_weight * tilt_weight + 0.04)
    mixed = own_part + tilt_weight[:, None, None, None] * common[None] + 0.2 * linked
    return scale_back[:, None, None, None] * mixed


def with_ends(values, key, smallest, high):
    longest = values.shape.index(max(values.shape))
    spots = []
    for shift in (0, 1):
        where = [jax.random.randint(jax.random.fold_in(key, axis), (), 0, length) for axis, length in enumerate(values.shape)]
        where[longest] = (where[longest] + shift) % values.shape[longest]
        spots.append(tuple(where))
    return values.at[spots[0]].set(smallest).at[spots[1]].set(high)


def level_of(rng, dims, pieces, least, top_value):
    loudness = 1.0
    for position, blocks in pieces:
        draws = jax.random.uniform(jax.random.fold_in(jax.random.fold_in(rng, 6), position), (blocks,), jnp.float32, least / len(pieces), top_value / len(pieces))
        loudness = loudness * jnp.repeat(jnp.exp(draws), dims[position] // blocks).reshape((-1,) + (1,) * (len(dims) - 1 - position))
    return loudness


def normal_values(key, dims, deviation, most, kind=jnp.bfloat16):
    return jnp.clip(deviation * jax.random.normal(key, dims, jnp.float32), -most, most).astype(kind)


def setup_inputs(seed: int = 0) -> dict:
    splits = jax.random.split(jax.random.key(seed), 10)
    return {
        "krylov_block": draw_krylov_block(jax.random.fold_in(splits[9], 71), 0),
        "prior_basis": draw_prior_basis(jax.random.fold_in(splits[9], 71), 0),
        "flux_along": normal_values(splits[2], (FIELDS, FIELDS), FIELDS ** -0.5, 1.25, jnp.float32),
        "flux_across": normal_values(splits[3], (FIELDS, FIELDS), FIELDS ** -0.5, 1.25, jnp.float32),
        "collision": jnp.clip(jnp.exp(math.log(10.0) - 2.3025851 * jax.random.uniform(splits[4], (NX, NY), jnp.float32) ** level_of(splits[4], (NX, NY), ((0, 8), (1, 4)), -0.2, 0.2)), 1.0, 10.0),
        "field_rates": jnp.clip(jnp.exp(jax.random.uniform(splits[5], (FIELDS,), jnp.float32, math.log(0.5), math.log(2.0))), 0.5, 2.0),
        "wall_table": jnp.clip(jax.random.uniform(splits[6], (TYPES, FIELDS), jnp.float32, 0.5, 3.0), 0.5, 3.0),
        "wall_mask": with_ends((jax.random.randint(splits[7], (NX, NY), 0, 4) < 1).astype(jnp.int32), jax.random.fold_in(splits[7], 1), 0, 1),
        "wall_type": with_ends(jax.random.randint(splits[8], (NX, NY), 0, TYPES), jax.random.fold_in(splits[8], 1), 0, TYPES - 1).astype(jnp.int32),
    }


damping = 0.0625
precise = lax.Precision.HIGHEST

def wall_gains(wall_mask, wall_type, wall_table):
    type_ids = jnp.arange(wall_table.shape[0], dtype=jnp.int32)
    onehot = (wall_type[None, :, :] == type_ids[:, None, None]).astype(jnp.float32)
    gains = jnp.einsum('txy,tf->fxy', onehot, wall_table, precision=precise)
    return gains * wall_mask.astype(jnp.float32)[None, :, :]

def operate_block(padded, local_coeff, flux_along, flux_across):
    rows_x = padded.shape[2] - 4
    rows_y = padded.shape[3] - 4

    def shifted(step_x, step_y):
        return padded[:, :, 2 + step_x:2 + step_x + rows_x, 2 + step_y:2 + step_y + rows_y]
    centre = shifted(0, 0)
    grad_x = 0.5 * (shifted(1, 0) - shifted(-1, 0))
    grad_y = 0.5 * (shifted(0, 1) - shifted(0, -1))
    fourth = shifted(-2, 0) - 4.0 * shifted(-1, 0) + 6.0 * centre - 4.0 * shifted(1, 0) + shifted(2, 0)
    fourth = fourth + shifted(0, -2) - 4.0 * shifted(0, -1) + 6.0 * centre - 4.0 * shifted(0, 1) + shifted(0, 2)
    result = local_coeff[None] * centre + damping * fourth
    result = result + jnp.einsum('fg,mgxy->mfxy', flux_along, grad_x, precision=precise)
    result = result + jnp.einsum('fg,mgxy->mfxy', flux_across, grad_y, precision=precise)
    return result

def inner_all(left, right):
    return jnp.einsum('kfxy,mfxy->km', left, right, precision=precise)

def mix_basis(weights, basis):
    return jnp.einsum('km,kfxy->mfxy', weights, basis, precision=precise)

def reference(krylov_block, prior_basis, flux_along, flux_across, collision, field_rates, wall_table, wall_mask, wall_type):
    inv_cells = 1.0 / (FIELDS * NX * NY)
    local_coeff = collision[None, :, :] * field_rates[:, None, None] + wall_gains(wall_mask, wall_type, wall_table)

    def apply_one(vector):
        padded = jnp.pad(vector[None], ((0, 0), (0, 0), (2, 2), (2, 2)))
        return operate_block(padded, local_coeff, flux_along, flux_across)[0]
    applied = lax.map(apply_one, krylov_block)
    first_pass = inner_all(prior_basis, applied) * inv_cells
    applied = applied - mix_basis(first_pass, prior_basis)
    second_pass = inner_all(prior_basis, applied) * inv_cells
    applied = applied - mix_basis(second_pass, prior_basis)
    projection = first_pass + second_pass
    identity_m = jnp.eye(BLOCK, dtype=jnp.float32)
    lower_one = jnp.linalg.cholesky(inner_all(applied, applied) * inv_cells)
    inv_one = jax.scipy.linalg.solve_triangular(lower_one, identity_m, lower=True)
    orthonormal = jnp.einsum('ij,jfxy->ifxy', inv_one, applied, precision=precise)
    lower_two = jnp.linalg.cholesky(inner_all(orthonormal, orthonormal) * inv_cells)
    inv_two = jax.scipy.linalg.solve_triangular(lower_two, identity_m, lower=True)
    new_block = jnp.einsum('ij,jfxy->ifxy', inv_two, orthonormal, precision=precise)
    triangle = jnp.dot(lower_one, lower_two, precision=precise).T
    return (new_block, projection, triangle)
```

```python
import functools

import jax
import jax.numpy as jnp
from jax import lax
from jax.experimental import pallas as pl
from jax.experimental.pallas import tpu as pltpu
from jax.sharding import PartitionSpec as P

damping = 0.0625
precise = lax.Precision.HIGHEST
f32, b16 = jnp.float32, jnp.bfloat16


def dot(a, b, precision=None):
    return lax.dot_general(
        a, b, (((1,), (0,)), ((), ())), precision=precision, preferred_element_type=f32
    )


def dot_t(a, b, precision=None):
    return lax.dot_general(
        a, b, (((1,), (1,)), ((), ())), precision=precision, preferred_element_type=f32
    )


def iota(shape, dim):
    return lax.broadcasted_iota(jnp.int32, shape, dim)


def pieces(a):
    high = a.astype(b16).astype(f32)
    rest = a - high
    mid = rest.astype(b16).astype(f32)
    return high, mid, (rest - mid).astype(b16).astype(f32)


def factor(a):
    size = a.shape[0]
    row, col = iota(a.shape, 0), iota(a.shape, 1)
    row1 = iota((size, 1), 0)
    inv = jnp.where(row == col, 1.0, 0.0).astype(f32)
    for j in range(size):
        scale = jnp.where(row1 > j, a[:, j : j + 1] / a[j : j + 1, j : j + 1], 0.0)
        inv = inv - scale * inv[j : j + 1, :]
        a = a - scale * a[j : j + 1, :]
    diag = jnp.sum(jnp.where(row == col, a, 0.0), axis=1, keepdims=True)
    root = 1.0 / jnp.sqrt(diag)
    return jnp.where(col >= row, a * root, 0.0), inv * root


def selector(count, width, start, levels):
    row, col = iota((count, width), 0), iota((count, width), 1)
    hit = col == row + start
    for level in range(1, levels):
        hit = hit | (col == row + (start + level * count))
    return jnp.where(hit, 1.0, 0.0).astype(f32)


def spread(parts, width):
    blocks = []
    for level in range(3):
        total = None
        for weights, start in parts:
            term = dot(
                pieces(weights)[level].astype(b16),
                selector(weights.shape[1], width, start, 3 - level).astype(b16),
            )
            total = term if total is None else total + term
        blocks.append(total)
    return jnp.concatenate(blocks, axis=0).astype(b16)


def fold_rows(a, count):
    return a[:count] + a[count : 2 * count] + a[2 * count : 3 * count]


def kernel(
    dims, inv_cells,
    kry, pri, along, across, coll, rates, table, wmask, wtype,
    out, proj_out, tri_out,
    kv, pv, vals, left, right, app, grad, kron_h, kron_l, stack, ortho, tile,
    y1, x1, y2, x2, local_sem, halo_send, halo_recv,
    y1s, y1r, x1s, x1r, y2s, y2r, x2s, x2r,
):
    m, k, nf, nx, ny, types = dims
    rows = nf * m
    block = 3 * m
    width = stack.shape[1]
    gx, gy = lax.axis_index("gx"), lax.axis_index("gy")
    px, py = lax.axis_size("gx"), lax.axis_size("gy")
    MESH = pl.DeviceIdType.MESH

    halves = ny // 128
    load_k = pltpu.make_async_copy(kry, kv, local_sem.at[0])
    load_p = pltpu.make_async_copy(pri, pv, local_sem.at[1])
    load_k.start()
    load_p.start()

    def lines(f, x, h, count):
        return pl.ds((f * halves + h) * nx + x, count, stride=nf * halves * nx)

    barrier = pltpu.get_barrier_semaphore()
    for axis, me, n in (("gy", gy, py), ("gx", gx, px)):
        for off in range(1, n):
            pl.semaphore_signal(
                barrier, inc=1, device_id={axis: lax.rem(me + off, n)}, device_id_type=MESH
            )
    pl.semaphore_wait(barrier, px + py - 2)

    load_k.wait()

    def to_rows(x):
        def body(f, carry):
            at = pl.multiple_of(f * m, m)
            for h in range(halves):
                lanes = pl.ds(h * 128, 128)
                vals[x + 2, pl.ds(at, m), lanes] = kv[lines(f, x, h, m), :]
            return carry

        lax.fori_loop(0, nf, body, 0, unroll=2)

    def remote(src, dst, index, where):
        return pltpu.make_async_remote_copy(
            src_ref=src, dst_ref=dst, send_sem=halo_send.at[index], recv_sem=halo_recv.at[index],
            device_id=where, device_id_type=MESH,
        )

    send_up = remote(vals.at[pl.ds(nx, 2)], vals.at[pl.ds(0, 2)], 0, {"gx": lax.rem(gx + 1, px)})
    send_down = remote(
        vals.at[pl.ds(2, 2)], vals.at[pl.ds(nx + 2, 2)], 1, {"gx": lax.rem(gx + px - 1, px)}
    )
    send_right = remote(
        vals.at[pl.ds(2, nx), :, pl.ds(ny - 128, 128)], left, 2, {"gy": lax.rem(gy + 1, py)}
    )
    send_left = remote(
        vals.at[pl.ds(2, nx), :, pl.ds(0, 128)], right, 3, {"gy": lax.rem(gy + py - 1, py)}
    )

    for x in (nx - 2, nx - 1):
        to_rows(x)
    pl.when(gx < px - 1)(send_up.start)
    for x in (0, 1):
        to_rows(x)
    pl.when(gx > 0)(send_down.start)

    def to_rows_inner(x, carry):
        to_rows(x)
        return carry

    lax.fori_loop(2, nx - 2, to_rows_inner, 0)
    pl.when(gy < py - 1)(send_right.start)
    pl.when(gy > 0)(send_left.start)

    @pl.when(gx == 0)
    def _():
        vals[0:2] = jnp.zeros((2, rows, ny), f32)

    @pl.when(gx == px - 1)
    def _():
        vals[nx + 2 : nx + 4] = jnp.zeros((2, rows, ny), f32)

    @pl.when(gy == 0)
    def _():
        left[...] = jnp.zeros(left.shape, f32)

    @pl.when(gy == py - 1)
    def _():
        right[...] = jnp.zeros(right.shape, f32)

    pick = jnp.where(iota((rows, nf), 0) // m == iota((rows, nf), 1), 1.0, 0.0).astype(f32)
    same = (iota((rows, rows), 0) % m) == (iota((rows, rows), 1) % m)
    for index, flux in enumerate((along, across)):
        full = jnp.where(same, dot_t(dot(pick, flux[...], precise), pick, precise), 0.0)
        high = full.astype(b16)
        kron_h[index] = high
        kron_l[index] = (full - high.astype(f32)).astype(b16)

    load_p.wait()

    def prior_step(i, total):
        x, f = i // nf, i % nf
        cols = []
        for h in range(halves):
            cols.append(pv[lines(f, x, h, k), :])
        p = jnp.concatenate(cols, axis=1)
        parts = list(pieces(p))
        pad = width - block - 3 * k
        if pad:
            parts.append(jnp.zeros((pad, ny), f32))
        both = jnp.concatenate(parts, axis=0).astype(b16)
        stack[i, block:width, :] = both
        return total + dot_t(both, both)

    basis = lax.fori_loop(
        0, nf * nx, prior_step, jnp.zeros((width - block, width - block), f32), unroll=2
    )
    tile[...] = jnp.zeros(tile.shape, f32)
    tile[m : m + k, 0 : width - block] = fold_rows(basis, k) * inv_cells

    def operate(x):
        row_c = jnp.broadcast_to(coll[pl.ds(x, 1), :], (m, ny))
        mask = wmask[pl.ds(x, 1), :].astype(f32)
        kind = wtype[pl.ds(x, 1), :]
        gains = [
            jnp.broadcast_to(jnp.where(kind == t, mask, 0.0), (m, ny)) for t in range(types)
        ]

        def body(f, carry):
            at = pl.ds(pl.multiple_of(f * m, m), m)
            v = vals[x + 2, at, :]
            coeff = row_c * rates[f]
            for t in range(types):
                coeff = coeff + gains[t] * table[t, f]
            b2, b1, a1, a2 = (vals[x + s, at, :] for s in (0, 1, 3, 4))
            ext = jnp.concatenate([left[x, at, :], v, right[x, at, :]], axis=1)
            span = ny + 256
            c2, c1, d1, d2 = (
                pltpu.roll(ext, s % span, 1)[:, 128 : 128 + ny] for s in (2, 1, -1, -2)
            )
            fourth = b2 - 4.0 * b1 + 6.0 * v - 4.0 * a1 + a2
            fourth = fourth + c2 - 4.0 * c1 + 6.0 * v - 4.0 * d1 + d2
            app[at, :] = coeff * v + damping * fourth
            for index, g in enumerate((0.5 * (a1 - b1), 0.5 * (d1 - c1))):
                high = g.astype(b16)
                grad[index, 0, at, :] = high
                grad[index, 1, at, :] = (g - high.astype(f32)).astype(b16)
            return carry

        lax.fori_loop(0, nf, body, 0, unroll=2)
        for index in range(2):
            high, low = grad[index, 0], grad[index, 1]
            app[...] += (
                dot(kron_h[index], high) + dot(kron_h[index], low) + dot(kron_l[index], high)
            )

    def gram(x, total):
        def body(f, total):
            a = app[pl.ds(pl.multiple_of(f * m, m), m), :]
            both = jnp.concatenate(pieces(a), axis=0).astype(b16)
            i = x * nf + f
            stack[i, 0:block, :] = both
            return total + dot_t(both, stack[i])

        return lax.fori_loop(0, nf, body, total, unroll=2)

    def row_step(x, total):
        operate(x)
        return gram(x, total)

    pl.when(gy > 0)(send_right.wait_recv)
    pl.when(gy < py - 1)(send_left.wait_recv)
    total = jnp.zeros((block, width), f32)
    total = lax.fori_loop(2, nx - 2, row_step, total)
    pl.when(gx > 0)(send_up.wait_recv)
    pl.when(gx < px - 1)(send_down.wait_recv)
    total = lax.fori_loop(
        0, 4, lambda j, t: row_step(j + (j // 2) * (nx - 4), t), total
    )

    def all_reduce(value, bufs):
        for axis, me, n, buf, ss, rs in bufs:
            buf[me] = value
            copies = []
            for off in range(1, n):
                copy = pltpu.make_async_remote_copy(
                    src_ref=buf.at[me], dst_ref=buf.at[me],
                    send_sem=ss.at[off - 1], recv_sem=rs.at[off - 1],
                    device_id={axis: lax.rem(me + off, n)}, device_id_type=MESH,
                )
                copy.start()
                copies.append(copy)
            for copy in copies:
                copy.wait()
            value = buf[0]
            for j in range(1, n):
                value = value + buf[j]
        return value

    tile[0:m, :] = fold_rows(total, m) * inv_cells
    sums = all_reduce(
        tile[...], (("gy", gy, py, y1, y1s, y1r), ("gx", gx, px, x1, x1s, x1r))
    )
    top = sums[0:m]
    own = dot_t(top, selector(m, width, 0, 3), precise)
    first = dot_t(top, selector(k, width, block, 3), precise)
    basis_gram = dot_t(sums[m : m + k], selector(k, width, 0, 3), precise)
    proj = first + (first - dot(first, basis_gram, precise))
    cross = dot_t(proj, first, precise)
    cross_t = dot_t(first, proj, precise)
    square = dot_t(dot(proj, basis_gram, precise), proj, precise)
    upper_one, inv_one = factor(own - cross - cross_t + square)
    eye = jnp.where(iota((k, k), 0) == iota((k, k), 1), 1.0, 0.0).astype(f32)
    proj_out[...] = dot_t(eye, proj, precise)

    mixing = spread(((inv_one, 0), (-dot(inv_one, proj, precise), block)), width)

    def mix_step(i, total):
        q = fold_rows(dot(mixing, stack[i]), m)
        both = jnp.concatenate(pieces(q), axis=0).astype(b16)
        ortho[i] = both
        return total + dot_t(both, both)

    second = lax.fori_loop(0, nf * nx, mix_step, jnp.zeros((block, block), f32), unroll=4)
    tile[0:m, 0:block] = fold_rows(second, m) * inv_cells
    tile[0:m, block:width] = jnp.zeros((m, width - block), f32)
    sums = all_reduce(
        tile[0:m, :], (("gy", gy, py, y2, y2s, y2r), ("gx", gx, px, x2, x2s, x2r))
    )
    upper_two, inv_two = factor(dot_t(sums, selector(m, width, 0, 3), precise))
    tri_out[...] = dot(upper_two, upper_one, precise)
    last = spread(((inv_two, 0),), block)

    def last_step(i, carry):
        x, f = i // nf, i % nf
        q = fold_rows(dot(last, ortho[i]), m)
        for h in range(halves):
            out[lines(f, x, h, m), :] = q[:, h * 128 : (h + 1) * 128]
        return carry

    lax.fori_loop(0, nf * nx, last_step, 0, unroll=4)

    pl.when(gx < px - 1)(send_up.wait_send)
    pl.when(gx > 0)(send_down.wait_send)
    pl.when(gy < py - 1)(send_right.wait_send)
    pl.when(gy > 0)(send_left.wait_send)


def in_tiles(a):
    n, f, x, y = a.shape
    return a.reshape(n, f, x, y // 128, 128).transpose(0, 1, 3, 2, 4).reshape(-1, 128)


def on_device(
    krylov_block, prior_basis, flux_along, flux_across, collision, field_rates,
    wall_table, wall_mask, wall_type,
):
    m, nf, nx, ny = krylov_block.shape
    k, types = prior_basis.shape[0], wall_table.shape[0]
    px, py = lax.axis_size("gx"), lax.axis_size("gy")
    inv_cells = 1.0 / (nf * nx * px * ny * py)
    block = 3 * m
    width = block + -(-3 * k // 16) * 16
    rows, halves = nf * m, ny // 128
    hbm = pl.BlockSpec(memory_space=pl.ANY)
    vmem = pl.BlockSpec(memory_space=pltpu.VMEM)
    smem = pl.BlockSpec(memory_space=pltpu.SMEM)
    sems = pltpu.SemaphoreType.DMA
    new, proj, tri = pl.pallas_call(
        functools.partial(kernel, (m, k, nf, nx, ny, types), inv_cells),
        out_shape=(
            jax.ShapeDtypeStruct((halves * m * nf * nx, 128), f32),
            jax.ShapeDtypeStruct((k, m), f32),
            jax.ShapeDtypeStruct((m, m), f32),
        ),
        in_specs=[hbm, hbm, vmem, vmem, vmem, smem, smem, vmem, vmem],
        out_specs=(vmem, vmem, vmem),
        scratch_shapes=[
            pltpu.VMEM((halves * m * nf * nx, 128), f32),
            pltpu.VMEM((halves * k * nf * nx, 128), f32),
            pltpu.VMEM((nx + 4, rows, ny), f32),
            pltpu.VMEM((nx, rows, 128), f32),
            pltpu.VMEM((nx, rows, 128), f32),
            pltpu.VMEM((rows, ny), f32),
            pltpu.VMEM((2, 2, rows, ny), b16),
            pltpu.VMEM((2, rows, rows), b16),
            pltpu.VMEM((2, rows, rows), b16),
            pltpu.VMEM((nf * nx, width, ny), b16),
            pltpu.VMEM((nf * nx, block, ny), b16),
            pltpu.VMEM((m + k, width), f32),
            pltpu.VMEM((py, m + k, width), f32),
            pltpu.VMEM((px, m + k, width), f32),
            pltpu.VMEM((py, m, width), f32),
            pltpu.VMEM((px, m, width), f32),
            sems((2,)), sems((4,)), sems((4,)),
            sems((py - 1,)), sems((py - 1,)), sems((px - 1,)), sems((px - 1,)),
            sems((py - 1,)), sems((py - 1,)), sems((px - 1,)), sems((px - 1,)),
        ],
        compiler_params=pltpu.CompilerParams(
            collective_id=0, has_side_effects=True, vmem_limit_bytes=60 * 1024 * 1024
        ),
    )(
        in_tiles(krylov_block), in_tiles(prior_basis), flux_along, flux_across, collision,
        field_rates, wall_table, wall_mask, wall_type,
    )
    new = new.reshape(m, nf, halves, nx, 128).transpose(0, 1, 3, 2, 4).reshape(m, nf, nx, ny)
    return (new, proj, tri)


def solution(mesh):
    placed = (
        P(None, None, "gx", "gy"), P(None, None, "gx", "gy"), P(), P(), P("gx", "gy"),
        P(), P(), P("gx", "gy"), P("gx", "gy"),
    )
    return jax.shard_map(
        on_device,
        mesh=mesh,
        in_specs=placed,
        out_specs=(P(None, None, "gx", "gy"), P(), P()),
        check_vma=False,
    )
```

```python
import functools

import jax
import jax.numpy as jnp
from jax import lax
from jax.experimental import pallas as pl
from jax.experimental.pallas import tpu as pltpu
from jax.sharding import PartitionSpec as P

damping = 0.0625
precise = lax.Precision.HIGHEST
f32, b16 = jnp.float32, jnp.bfloat16


def dot(a, b, precision=None):
    return lax.dot_general(
        a, b, (((1,), (0,)), ((), ())), precision=precision, preferred_element_type=f32
    )


def dot_t(a, b, precision=None):
    return lax.dot_general(
        a, b, (((1,), (1,)), ((), ())), precision=precision, preferred_element_type=f32
    )


def iota(shape, dim):
    return lax.broadcasted_iota(jnp.int32, shape, dim)


def pieces(a):
    high = a.astype(b16).astype(f32)
    rest = a - high
    mid = rest.astype(b16).astype(f32)
    return high, mid, (rest - mid).astype(b16).astype(f32)


def factor(a):
    size = a.shape[0]
    row, col = iota(a.shape, 0), iota(a.shape, 1)
    row1 = iota((size, 1), 0)
    inv = jnp.where(row == col, 1.0, 0.0).astype(f32)
    for j in range(size):
        scale = jnp.where(row1 > j, a[:, j : j + 1] / a[j : j + 1, j : j + 1], 0.0)
        inv = inv - scale * inv[j : j + 1, :]
        a = a - scale * a[j : j + 1, :]
    diag = jnp.sum(jnp.where(row == col, a, 0.0), axis=1, keepdims=True)
    root = 1.0 / jnp.sqrt(diag)
    return jnp.where(col >= row, a * root, 0.0), inv * root


def where01(hit):
    return jnp.where(hit, 1.0, 0.0).astype(f32)


def spread(parts, levels, groups, group_of):
    blocks = []
    for level in range(levels):
        total = None
        for weights, pick in parts:
            term = dot(pieces(weights)[level].astype(b16), pick(level).astype(b16))
            total = term if total is None else total + term
        for group in range(groups):
            blocks.append(jnp.where(group_of == group, total, 0.0))
    return jnp.concatenate(blocks, axis=0).astype(b16)


def fold_rows(a, count):
    total = a[:count]
    for start in range(count, a.shape[0], count):
        total = total + a[start : start + count]
    return total


def kernel(
    dims, inv_cells,
    kry, pri, along, across, coll, rates, table, wmask, wtype,
    out, proj_out, tri_out,
    kv, pv, vals, left, right, low_x, high_x, app, grad, kron_h, kron_l, stack, ortho, tile,
    y1, x1, y2, x2, local_sem, halo_send, halo_recv,
    y1s, y1r, x1s, x1r, y2s, y2r, x2s, x2r,
):
    m, k, nf, nx, ny, types = dims
    rows = nf * m
    steps = nf * nx
    own3 = 6 * m
    pad_k = (stack.shape[1] - own3) // 2
    gx, gy = lax.axis_index("gx"), lax.axis_index("gy")
    px, py = lax.axis_size("gx"), lax.axis_size("gy")
    MESH = pl.DeviceIdType.MESH

    halves = ny // 128
    load_k = pltpu.make_async_copy(kry, kv, local_sem.at[0])
    load_p = pltpu.make_async_copy(pri, pv, local_sem.at[1])
    load_k.start()
    load_p.start()

    def lines(f, x, h, count):
        return pl.ds((f * halves + h) * nx + x, count, stride=nf * halves * nx)

    barrier = pltpu.get_barrier_semaphore()
    for axis, me, n in (("gy", gy, py), ("gx", gx, px)):
        for off in range(1, n):
            pl.semaphore_signal(
                barrier, inc=1, device_id={axis: lax.rem(me + off, n)}, device_id_type=MESH
            )
    pl.semaphore_wait(barrier, px + py - 2)

    load_k.wait()

    def to_rows(x):
        def body(f, carry):
            at = pl.multiple_of(f * m, m)
            for h in range(halves):
                lanes = pl.ds(h * 128, 128)
                vals[x + 2, pl.ds(at, m), lanes] = kv[lines(f, x, h, m), :]
            return carry

        lax.fori_loop(0, nf, body, 0, unroll=2)

    def remote(src, dst, index, where):
        return pltpu.make_async_remote_copy(
            src_ref=src, dst_ref=dst, send_sem=halo_send.at[index], recv_sem=halo_recv.at[index],
            device_id=where, device_id_type=MESH,
        )

    send_up = remote(vals.at[pl.ds(nx, 2)], low_x, 0, {"gx": lax.rem(gx + 1, px)})
    send_down = remote(
        vals.at[pl.ds(2, 2)], high_x, 1, {"gx": lax.rem(gx + px - 1, px)}
    )
    send_right = remote(
        vals.at[pl.ds(2, nx), :, pl.ds(ny - 128, 128)], left, 2, {"gy": lax.rem(gy + 1, py)}
    )
    send_left = remote(
        vals.at[pl.ds(2, nx), :, pl.ds(0, 128)], right, 3, {"gy": lax.rem(gy + py - 1, py)}
    )

    for x in (nx - 2, nx - 1):
        to_rows(x)
    pl.when(gx < px - 1)(send_up.start)
    for x in (0, 1):
        to_rows(x)
    pl.when(gx > 0)(send_down.start)

    def to_rows_inner(x, carry):
        to_rows(x)
        return carry

    lax.fori_loop(2, nx - 2, to_rows_inner, 0)
    pl.when(gy < py - 1)(send_right.start)
    pl.when(gy > 0)(send_left.start)

    vals[0:2] = jnp.zeros((2, rows, ny), f32)
    vals[nx + 2 : nx + 4] = jnp.zeros((2, rows, ny), f32)

    @pl.when(gy == 0)
    def _():
        left[...] = jnp.zeros(left.shape, f32)

    @pl.when(gy == py - 1)
    def _():
        right[...] = jnp.zeros(right.shape, f32)

    pick = jnp.where(iota((rows, nf), 0) // m == iota((rows, nf), 1), 1.0, 0.0).astype(f32)
    same = (iota((rows, rows), 0) % m) == (iota((rows, rows), 1) % m)
    for index, flux in enumerate((along, across)):
        full = jnp.where(same, dot_t(dot(pick, flux[...], precise), pick, precise), 0.0)
        high = full.astype(b16)
        kron_h[index] = high
        kron_l[index] = (full - high.astype(f32)).astype(b16)

    load_p.wait()

    def prior_step(pair, total):
        pairs = []
        for half in range(2):
            i = 2 * pair + half
            x, f = i // nf, i % nf
            p = jnp.concatenate([pv[lines(f, x, h, k), :] for h in range(halves)], axis=1)
            parts = list(pieces(p))
            if pad_k > 3 * k:
                parts.append(jnp.zeros((pad_k - 3 * k, ny), f32))
            both = jnp.concatenate(parts, axis=0).astype(b16)
            start = own3 + half * pad_k
            stack[pair, start : start + pad_k, :] = both
            pairs.append(both[0 : 2 * k])
        both = jnp.concatenate(pairs, axis=0)
        return total + dot_t(both, both)

    basis = lax.fori_loop(
        0, steps // 2, prior_step, jnp.zeros((4 * k, 4 * k), f32), unroll=4
    )
    wide = (4 * k, 4 * k)
    basis = jnp.where(iota(wide, 0) // (2 * k) == iota(wide, 1) // (2 * k), basis, 0.0)
    pick_k = where01(iota((k, 4 * k), 1) % k == iota((k, 4 * k), 0))
    tile[...] = jnp.zeros(tile.shape, f32)
    tile[m : m + k, 0:k] = dot_t(fold_rows(basis, k), pick_k, precise) * inv_cells

    def operate(x, carry_x):
        row_c = jnp.broadcast_to(coll[pl.ds(x, 1), :], (m, ny))
        mask = wmask[pl.ds(x, 1), :].astype(f32)
        kind = wtype[pl.ds(x, 1), :]
        gains = [
            jnp.broadcast_to(jnp.where(kind == t, mask, 0.0), (m, ny)) for t in range(types)
        ]

        def body(f, carry):
            at = pl.ds(pl.multiple_of(f * m, m), m)
            v = vals[x + 2, at, :]
            coeff = row_c * rates[f]
            for t in range(types):
                coeff = coeff + gains[t] * table[t, f]
            b2, b1, a1, a2 = (vals[x + s, at, :] for s in (0, 1, 3, 4))
            ext = jnp.concatenate([left[x, at, :], v, right[x, at, :]], axis=1)
            span = ny + 256
            c2, c1, d1, d2 = (
                pltpu.roll(ext, s % span, 1)[:, 128 : 128 + ny] for s in (2, 1, -1, -2)
            )
            fourth = b2 - 4.0 * b1 + 6.0 * v - 4.0 * a1 + a2
            fourth = fourth + c2 - 4.0 * c1 + 6.0 * v - 4.0 * d1 + d2
            app[x, at, :] = coeff * v + damping * fourth
            for index, g in enumerate((0.5 * (a1 - b1), 0.5 * (d1 - c1))):
                high = g.astype(b16)
                grad[index, 0, at, :] = high
                grad[index, 1, at, :] = (g - high.astype(f32)).astype(b16)
            return carry

        lax.fori_loop(0, nf, body, 0, unroll=2)
        for index in range(2):
            high, low = grad[index, 0], grad[index, 1]
            app[x] += dot(kron_h[index], high) + dot(kron_h[index], low) + dot(kron_l[index], high)
        return carry_x

    def gram(x, total):
        def body(t, total):
            a = app[x, pl.ds(pl.multiple_of(t * 2 * m, 2 * m), 2 * m), :]
            both = jnp.concatenate(pieces(a), axis=0).astype(b16)
            pair = x * (nf // 2) + t
            stack[pair, 0:own3, :] = both
            own = both[0 : 4 * m]
            right_side = [own]
            for half in range(2):
                start = own3 + half * pad_k
                right_side.append(stack[pair, start : start + 2 * k, :])
            return total + dot_t(own, jnp.concatenate(right_side, axis=0))

        return lax.fori_loop(0, nf // 2, body, total, unroll=nf // 2)

    pl.when(gy > 0)(send_right.wait_recv)
    pl.when(gy < py - 1)(send_left.wait_recv)
    lax.fori_loop(0, nx, operate, 0)
    total = jnp.zeros((4 * m, 4 * m + 4 * k), f32)
    total = lax.fori_loop(2, nx - 2, gram, total)

    def add_halo(near, far, x_near, x_far, sign):
        def body(f, carry):
            at = pl.ds(pl.multiple_of(f * m, m), m)
            v = near[at, :]
            app[x_near, at, :] += damping * (far[at, :] - 4.0 * v)
            app[x_far, at, :] += damping * v
            g = (0.5 * sign) * v
            high = g.astype(b16)
            grad[0, 0, at, :] = high
            grad[0, 1, at, :] = (g - high.astype(f32)).astype(b16)
            return carry

        lax.fori_loop(0, nf, body, 0, unroll=2)
        high, low = grad[0, 0], grad[0, 1]
        app[x_near] += dot(kron_h[0], high) + dot(kron_h[0], low) + dot(kron_l[0], high)

    @pl.when(gx > 0)
    def _():
        send_up.wait_recv()
        add_halo(low_x.at[1], low_x.at[0], 0, 1, -1.0)

    @pl.when(gx < px - 1)
    def _():
        send_down.wait_recv()
        add_halo(high_x.at[0], high_x.at[1], nx - 1, nx - 2, 1.0)

    total = lax.fori_loop(0, 4, lambda j, t: gram(j + (j // 2) * (nx - 4), t), total)

    def all_reduce(value, bufs):
        for axis, me, n, buf, ss, rs in bufs:
            buf[me] = value
            copies = []
            for off in range(1, n):
                copy = pltpu.make_async_remote_copy(
                    src_ref=buf.at[me], dst_ref=buf.at[me],
                    send_sem=ss.at[off - 1], recv_sem=rs.at[off - 1],
                    device_id={axis: lax.rem(me + off, n)}, device_id_type=MESH,
                )
                copy.start()
                copies.append(copy)
            for copy in copies:
                copy.wait()
            value = buf[0]
            for j in range(1, n):
                value = value + buf[j]
        return value

    total = fold_rows(total, 2 * m)
    col = iota(total.shape, 1)
    group = jnp.where(col < 4 * m, (col // m) % 2, (col - 4 * m) // (2 * k))
    total = fold_rows(jnp.where(group == iota(total.shape, 0) // m, total, 0.0), m)
    shape = (4 * m + 4 * k, tile.shape[1])
    row, col = iota(shape, 0), iota(shape, 1)
    fold = where01(col == jnp.where(row < 4 * m, row % m, m + (row - 4 * m) % k))
    tile[0:m, :] = dot(total, fold, precise) * inv_cells
    sums = all_reduce(
        tile[...], (("gy", gy, py, y1, y1s, y1r), ("gx", gx, px, x1, x1s, x1r))
    )
    top = sums[0:m]
    own, first = top[:, 0:m], top[:, m : m + k]
    basis_gram = sums[m : m + k, 0:k]
    proj = first + (first - dot(first, basis_gram, precise))
    cross = dot_t(proj, first, precise)
    cross_t = dot_t(first, proj, precise)
    square = dot_t(dot(proj, basis_gram, precise), proj, precise)
    upper_one, inv_one = factor(own - cross - cross_t + square)
    proj_out[...] = proj

    depth = stack.shape[1]

    def pick_own(level):
        row, col = iota((m, depth), 0), iota((m, depth), 1)
        return where01((col % m == row) & (col < (3 - level) * 2 * m))

    def pick_prior(level):
        row, col = iota((k, depth), 0), iota((k, depth), 1)
        at = (col + (pad_k - own3 % pad_k)) % pad_k
        return where01((at % k == row) & (at < (3 - level) * k) & (col >= own3))

    col = iota((m, depth), 1)
    group = jnp.where(col < own3, (col // m) % 2, jnp.where(col < own3 + pad_k, 0, 1))
    mixing = spread(
        ((inv_one, pick_own), (-dot(inv_one, proj, precise), pick_prior)), 3, 2, group
    )

    def mix_step(step, total):
        for half in range(2):
            q = jnp.concatenate(
                [
                    fold_rows(dot(mixing, stack[4 * step + 2 * half + j]), 2 * m)
                    for j in range(2)
                ],
                axis=0,
            )
            both = jnp.concatenate(pieces(q)[:2], axis=0).astype(b16)
            ortho[step, half * 8 * m : (half + 1) * 8 * m, :] = both
            total = total + dot_t(both, both)
        return total

    second = lax.fori_loop(
        0, steps // 8, mix_step, jnp.zeros((8 * m, 8 * m), f32), unroll=2
    )
    second = fold_rows(second, 4 * m)
    col = iota(second.shape, 1)
    second = jnp.where((col // m) % 4 == iota(second.shape, 0) // m, second, 0.0)
    sums = all_reduce(
        fold_rows(second, m) * inv_cells,
        (("gy", gy, py, y2, y2s, y2r), ("gx", gx, px, x2, x2s, x2r)),
    )
    pick_m = where01(iota(sums.shape, 1) % m == iota(sums.shape, 0))
    upper_two, inv_two = factor(dot_t(sums, pick_m, precise))
    tri_out[...] = dot(upper_two, upper_one, precise)

    def pick_two(level):
        row, col = iota((m, 16 * m), 0), iota((m, 16 * m), 1)
        return where01((col % m == row) & ((col // (4 * m)) % 2 < 2 - level))

    col = iota((m, 16 * m), 1)
    last = spread(((inv_two, pick_two),), 2, 8, (col // (8 * m)) * 4 + (col // m) % 4)

    def last_step(step, carry):
        q = fold_rows(dot(last, ortho[step]), 8 * m)
        for g in range(8):
            i = 8 * step + g
            x, f = i // nf, i % nf
            for h in range(halves):
                out[lines(f, x, h, m), :] = q[g * m : (g + 1) * m, h * 128 : (h + 1) * 128]
        return carry

    lax.fori_loop(0, steps // 8, last_step, 0, unroll=2)

    pl.when(gx < px - 1)(send_up.wait_send)
    pl.when(gx > 0)(send_down.wait_send)
    pl.when(gy < py - 1)(send_right.wait_send)
    pl.when(gy > 0)(send_left.wait_send)


def in_tiles(a):
    n, f, x, y = a.shape
    return a.reshape(n, f, x, y // 128, 128).transpose(0, 1, 3, 2, 4).reshape(-1, 128)


def on_device(
    krylov_block, prior_basis, flux_along, flux_across, collision, field_rates,
    wall_table, wall_mask, wall_type,
):
    m, nf, nx, ny = krylov_block.shape
    k, types = prior_basis.shape[0], wall_table.shape[0]
    px, py = lax.axis_size("gx"), lax.axis_size("gy")
    inv_cells = 1.0 / (nf * nx * px * ny * py)
    depth = 6 * m + 2 * (-(-3 * k // 16) * 16)
    steps, width = nf * nx, 8 * m
    rows, halves = nf * m, ny // 128
    hbm = pl.BlockSpec(memory_space=pl.ANY)
    vmem = pl.BlockSpec(memory_space=pltpu.VMEM)
    smem = pl.BlockSpec(memory_space=pltpu.SMEM)
    sems = pltpu.SemaphoreType.DMA
    new, proj, tri = pl.pallas_call(
        functools.partial(kernel, (m, k, nf, nx, ny, types), inv_cells),
        out_shape=(
            jax.ShapeDtypeStruct((halves * m * nf * nx, 128), f32),
            jax.ShapeDtypeStruct((m, k), f32),
            jax.ShapeDtypeStruct((m, m), f32),
        ),
        in_specs=[hbm, hbm, vmem, vmem, vmem, smem, smem, vmem, vmem],
        out_specs=(vmem, vmem, vmem),
        scratch_shapes=[
            pltpu.VMEM((halves * m * nf * nx, 128), f32),
            pltpu.VMEM((halves * k * nf * nx, 128), f32),
            pltpu.VMEM((nx + 4, rows, ny), f32),
            pltpu.VMEM((nx, rows, 128), f32),
            pltpu.VMEM((nx, rows, 128), f32),
            pltpu.VMEM((2, rows, ny), f32),
            pltpu.VMEM((2, rows, ny), f32),
            pltpu.VMEM((nx, rows, ny), f32),
            pltpu.VMEM((2, 2, rows, ny), b16),
            pltpu.VMEM((2, rows, rows), b16),
            pltpu.VMEM((2, rows, rows), b16),
            pltpu.VMEM((steps // 2, depth, ny), b16),
            pltpu.VMEM((steps // 8, 16 * m, ny), b16),
            pltpu.VMEM((m + k, width), f32),
            pltpu.VMEM((py, m + k, width), f32),
            pltpu.VMEM((px, m + k, width), f32),
            pltpu.VMEM((py, m, width), f32),
            pltpu.VMEM((px, m, width), f32),
            sems((2,)), sems((4,)), sems((4,)),
            sems((py - 1,)), sems((py - 1,)), sems((px - 1,)), sems((px - 1,)),
            sems((py - 1,)), sems((py - 1,)), sems((px - 1,)), sems((px - 1,)),
        ],
        compiler_params=pltpu.CompilerParams(
            collective_id=0, has_side_effects=True, vmem_limit_bytes=60 * 1024 * 1024
        ),
    )(
        in_tiles(krylov_block), in_tiles(prior_basis), flux_along, flux_across, collision,
        field_rates, wall_table, wall_mask, wall_type,
    )
    new = new.reshape(m, nf, halves, nx, 128).transpose(0, 1, 3, 2, 4).reshape(m, nf, nx, ny)
    return (new, proj.T, tri)


def solution(mesh):
    placed = (
        P(None, None, "gx", "gy"), P(None, None, "gx", "gy"), P(), P(), P("gx", "gy"),
        P(), P(), P("gx", "gy"), P("gx", "gy"),
    )
    return jax.shard_map(
        on_device,
        mesh=mesh,
        in_specs=placed,
        out_specs=(P(None, None, "gx", "gy"), P(), P()),
        check_vma=False,
    )
```

```python
import functools

import jax
import jax.numpy as jnp
from jax import lax
from jax.experimental import pallas as pl
from jax.experimental.pallas import tpu as pltpu
from jax.sharding import PartitionSpec as P

damping = 0.0625
precise = lax.Precision.HIGHEST
f32, b16 = jnp.float32, jnp.bfloat16


def dot(a, b, precision=None):
    return lax.dot_general(
        a, b, (((1,), (0,)), ((), ())), precision=precision, preferred_element_type=f32
    )


def dot_t(a, b, precision=None):
    return lax.dot_general(
        a, b, (((1,), (1,)), ((), ())), precision=precision, preferred_element_type=f32
    )


def iota(shape, dim):
    return lax.broadcasted_iota(jnp.int32, shape, dim)


def pieces(a):
    high = a.astype(b16).astype(f32)
    rest = a - high
    mid = rest.astype(b16).astype(f32)
    return high, mid, (rest - mid).astype(b16).astype(f32)


def factor(a):
    size = a.shape[0]
    row, col = iota(a.shape, 0), iota(a.shape, 1)
    row1 = iota((size, 1), 0)
    inv = jnp.where(row == col, 1.0, 0.0).astype(f32)
    for j in range(size):
        scale = jnp.where(row1 > j, a[:, j : j + 1] / a[j : j + 1, j : j + 1], 0.0)
        inv = inv - scale * inv[j : j + 1, :]
        a = a - scale * a[j : j + 1, :]
    diag = jnp.sum(jnp.where(row == col, a, 0.0), axis=1, keepdims=True)
    root = 1.0 / jnp.sqrt(diag)
    return jnp.where(col >= row, a * root, 0.0), inv * root


def where01(hit):
    return jnp.where(hit, 1.0, 0.0).astype(f32)


def spread(parts, levels, groups, group_of):
    blocks = []
    for level in range(levels):
        total = None
        for weights, pick in parts:
            term = dot(pieces(weights)[level].astype(b16), pick(level).astype(b16))
            total = term if total is None else total + term
        for group in range(groups):
            blocks.append(jnp.where(group_of == group, total, 0.0))
    return jnp.concatenate(blocks, axis=0).astype(b16)


def fold_rows(a, count):
    total = a[:count]
    for start in range(count, a.shape[0], count):
        total = total + a[start : start + count]
    return total


def kernel(
    dims, inv_cells,
    kry, pri, along, across, coll, rates, table, wmask, wtype,
    out, proj_out, tri_out,
    kv, pv, vals, left, right, low_x, high_x, app, grad, kron_h, kron_l, stack, ortho, tile,
    y1, x1, y2, x2, local_sem, halo_send, halo_recv,
    y1s, y1r, x1s, x1r, y2s, y2r, x2s, x2r,
):
    m, k, nf, nx, ny, types = dims
    rows = nf * m
    steps = nf * nx
    own3 = 6 * m
    pad_k = (stack.shape[1] - own3) // 2
    gx, gy = lax.axis_index("gx"), lax.axis_index("gy")
    px, py = lax.axis_size("gx"), lax.axis_size("gy")
    MESH = pl.DeviceIdType.MESH

    halves = ny // 128
    load_k = pltpu.make_async_copy(kry, kv, local_sem.at[0])
    load_p = pltpu.make_async_copy(pri, pv, local_sem.at[1])
    load_k.start()
    load_p.start()

    def lines(f, x, h, count):
        return pl.ds((f * halves + h) * nx + x, count, stride=nf * halves * nx)

    barrier = pltpu.get_barrier_semaphore()
    for axis, me, n in (("gy", gy, py), ("gx", gx, px)):
        for off in range(1, n):
            pl.semaphore_signal(
                barrier, inc=1, device_id={axis: lax.rem(me + off, n)}, device_id_type=MESH
            )
    pl.semaphore_wait(barrier, px + py - 2)

    load_k.wait()

    def to_rows(x):
        def body(f, carry):
            at = pl.multiple_of(f * m, m)
            for h in range(halves):
                lanes = pl.ds(h * 128, 128)
                vals[x + 2, pl.ds(at, m), lanes] = kv[lines(f, x, h, m), :]
            return carry

        lax.fori_loop(0, nf, body, 0, unroll=nf // 2)

    def remote(src, dst, index, where):
        return pltpu.make_async_remote_copy(
            src_ref=src, dst_ref=dst, send_sem=halo_send.at[index], recv_sem=halo_recv.at[index],
            device_id=where, device_id_type=MESH,
        )

    send_up = remote(vals.at[pl.ds(nx, 2)], low_x, 0, {"gx": lax.rem(gx + 1, px)})
    send_down = remote(
        vals.at[pl.ds(2, 2)], high_x, 1, {"gx": lax.rem(gx + px - 1, px)}
    )
    send_right = remote(
        vals.at[pl.ds(2, nx), :, pl.ds(ny - 128, 128)], left, 2, {"gy": lax.rem(gy + 1, py)}
    )
    send_left = remote(
        vals.at[pl.ds(2, nx), :, pl.ds(0, 128)], right, 3, {"gy": lax.rem(gy + py - 1, py)}
    )

    for x in (nx - 2, nx - 1):
        to_rows(x)
    pl.when(gx < px - 1)(send_up.start)
    for x in (0, 1):
        to_rows(x)
    pl.when(gx > 0)(send_down.start)

    def to_rows_inner(x, carry):
        to_rows(x)
        return carry

    lax.fori_loop(2, nx - 2, to_rows_inner, 0)
    pl.when(gy < py - 1)(send_right.start)
    pl.when(gy > 0)(send_left.start)

    vals[0:2] = jnp.zeros((2, rows, ny), f32)
    vals[nx + 2 : nx + 4] = jnp.zeros((2, rows, ny), f32)

    @pl.when(gy == 0)
    def _():
        left[...] = jnp.zeros(left.shape, f32)

    @pl.when(gy == py - 1)
    def _():
        right[...] = jnp.zeros(right.shape, f32)

    pick = jnp.where(iota((rows, nf), 0) // m == iota((rows, nf), 1), 1.0, 0.0).astype(f32)
    same = (iota((rows, rows), 0) % m) == (iota((rows, rows), 1) % m)
    for index, flux in enumerate((along, across)):
        full = jnp.where(same, dot_t(dot(pick, flux[...], precise), pick, precise), 0.0)
        high = full.astype(b16)
        kron_h[index] = high
        kron_l[index] = (full - high.astype(f32)).astype(b16)

    load_p.wait()

    def prior_step(pair, total):
        pairs = []
        for half in range(2):
            i = 2 * pair + half
            x, f = i // nf, i % nf
            p = jnp.concatenate([pv[lines(f, x, h, k), :] for h in range(halves)], axis=1)
            parts = list(pieces(p))
            if pad_k > 3 * k:
                parts.append(jnp.zeros((pad_k - 3 * k, ny), f32))
            both = jnp.concatenate(parts, axis=0).astype(b16)
            start = own3 + half * pad_k
            stack[pair, start : start + pad_k, :] = both
            pairs.append(both[0 : 2 * k])
        both = jnp.concatenate(pairs, axis=0)
        return total + dot_t(both, both)

    basis = lax.fori_loop(
        0, steps // 2, prior_step, jnp.zeros((4 * k, 4 * k), f32), unroll=4
    )
    wide = (4 * k, 4 * k)
    basis = jnp.where(iota(wide, 0) // (2 * k) == iota(wide, 1) // (2 * k), basis, 0.0)
    pick_k = where01(iota((k, 4 * k), 1) % k == iota((k, 4 * k), 0))
    tile[...] = jnp.zeros(tile.shape, f32)
    tile[m : m + k, 0:k] = dot_t(fold_rows(basis, k), pick_k, precise) * inv_cells

    def operate(x, carry_x):
        row_c = jnp.broadcast_to(coll[pl.ds(x, 1), :], (m, ny))
        mask = wmask[pl.ds(x, 1), :].astype(f32)
        kind = wtype[pl.ds(x, 1), :]
        gains = [
            jnp.broadcast_to(jnp.where(kind == t, mask, 0.0), (m, ny)) for t in range(types)
        ]

        def body(f, carry):
            at = pl.ds(pl.multiple_of(f * m, m), m)
            v = vals[x + 2, at, :]
            coeff = row_c * rates[f]
            for t in range(types):
                coeff = coeff + gains[t] * table[t, f]
            b2, b1, a1, a2 = (vals[x + s, at, :] for s in (0, 1, 3, 4))
            ext = jnp.concatenate([left[x, at, :], v, right[x, at, :]], axis=1)
            span = ny + 256
            c2, c1, d1, d2 = (
                pltpu.roll(ext, s % span, 1)[:, 128 : 128 + ny] for s in (2, 1, -1, -2)
            )
            fourth = b2 - 4.0 * b1 + 6.0 * v - 4.0 * a1 + a2
            fourth = fourth + c2 - 4.0 * c1 + 6.0 * v - 4.0 * d1 + d2
            app[x, at, :] = coeff * v + damping * fourth
            for index, g in enumerate((0.5 * (a1 - b1), 0.5 * (d1 - c1))):
                high = g.astype(b16)
                grad[index, 0, at, :] = high
                grad[index, 1, at, :] = (g - high.astype(f32)).astype(b16)
            return carry

        lax.fori_loop(0, nf, body, 0, unroll=nf // 2)
        for index in range(2):
            high, low = grad[index, 0], grad[index, 1]
            app[x] += dot(kron_h[index], high) + dot(kron_h[index], low) + dot(kron_l[index], high)
        return carry_x

    def gram(x, total):
        def body(t, total):
            a = app[x, pl.ds(pl.multiple_of(t * 2 * m, 2 * m), 2 * m), :]
            both = jnp.concatenate(pieces(a), axis=0).astype(b16)
            pair = x * (nf // 2) + t
            stack[pair, 0:own3, :] = both
            own = both[0 : 4 * m]
            right_side = [own]
            for half in range(2):
                start = own3 + half * pad_k
                right_side.append(stack[pair, start : start + 2 * k, :])
            return total + dot_t(own, jnp.concatenate(right_side, axis=0))

        return lax.fori_loop(0, nf // 2, body, total, unroll=nf // 2)

    pl.when(gy > 0)(send_right.wait_recv)
    pl.when(gy < py - 1)(send_left.wait_recv)
    lax.fori_loop(0, nx, operate, 0)
    total = jnp.zeros((4 * m, 4 * m + 4 * k), f32)
    total = lax.fori_loop(2, nx - 2, gram, total)

    def add_halo(near, far, x_near, x_far, sign):
        def body(f, carry):
            at = pl.ds(pl.multiple_of(f * m, m), m)
            v = near[at, :]
            app[x_near, at, :] += damping * (far[at, :] - 4.0 * v)
            app[x_far, at, :] += damping * v
            g = (0.5 * sign) * v
            high = g.astype(b16)
            grad[0, 0, at, :] = high
            grad[0, 1, at, :] = (g - high.astype(f32)).astype(b16)
            return carry

        lax.fori_loop(0, nf, body, 0, unroll=nf // 2)
        high, low = grad[0, 0], grad[0, 1]
        app[x_near] += dot(kron_h[0], high) + dot(kron_h[0], low) + dot(kron_l[0], high)

    @pl.when(gx > 0)
    def _():
        send_up.wait_recv()
        add_halo(low_x.at[1], low_x.at[0], 0, 1, -1.0)

    @pl.when(gx < px - 1)
    def _():
        send_down.wait_recv()
        add_halo(high_x.at[0], high_x.at[1], nx - 1, nx - 2, 1.0)

    total = lax.fori_loop(0, 4, lambda j, t: gram(j + (j // 2) * (nx - 4), t), total)

    def all_reduce(value, bufs):
        for axis, me, n, buf, ss, rs in bufs:
            buf[me] = value
            copies = []
            for off in range(1, n):
                copy = pltpu.make_async_remote_copy(
                    src_ref=buf.at[me], dst_ref=buf.at[me],
                    send_sem=ss.at[off - 1], recv_sem=rs.at[off - 1],
                    device_id={axis: lax.rem(me + off, n)}, device_id_type=MESH,
                )
                copy.start()
                copies.append(copy)
            for copy in copies:
                copy.wait()
            value = buf[0]
            for j in range(1, n):
                value = value + buf[j]
        return value

    total = fold_rows(total, 2 * m)
    col = iota(total.shape, 1)
    group = jnp.where(col < 4 * m, (col // m) % 2, (col - 4 * m) // (2 * k))
    total = fold_rows(jnp.where(group == iota(total.shape, 0) // m, total, 0.0), m)
    shape = (4 * m + 4 * k, tile.shape[1])
    row, col = iota(shape, 0), iota(shape, 1)
    fold = where01(col == jnp.where(row < 4 * m, row % m, m + (row - 4 * m) % k))
    tile[0:m, :] = dot(total, fold, precise) * inv_cells
    sums = all_reduce(
        tile[...], (("gy", gy, py, y1, y1s, y1r), ("gx", gx, px, x1, x1s, x1r))
    )
    top = sums[0:m]
    own, first = top[:, 0:m], top[:, m : m + k]
    basis_gram = sums[m : m + k, 0:k]
    proj = first + (first - dot(first, basis_gram, precise))
    cross = dot_t(proj, first, precise)
    cross_t = dot_t(first, proj, precise)
    square = dot_t(dot(proj, basis_gram, precise), proj, precise)
    upper_one, inv_one = factor(own - cross - cross_t + square)
    proj_out[...] = proj

    depth = stack.shape[1]

    def pick_own(level):
        row, col = iota((m, depth), 0), iota((m, depth), 1)
        return where01((col % m == row) & (col < (3 - level) * 2 * m))

    def pick_prior(level):
        row, col = iota((k, depth), 0), iota((k, depth), 1)
        at = (col + (pad_k - own3 % pad_k)) % pad_k
        return where01((at % k == row) & (at < (3 - level) * k) & (col >= own3))

    col = iota((m, depth), 1)
    group = jnp.where(col < own3, (col // m) % 2, jnp.where(col < own3 + pad_k, 0, 1))
    mixing = spread(
        ((inv_one, pick_own), (-dot(inv_one, proj, precise), pick_prior)), 3, 2, group
    )

    def mix_step(step, total):
        for half in range(2):
            q = jnp.concatenate(
                [
                    fold_rows(dot(mixing, stack[4 * step + 2 * half + j]), 2 * m)
                    for j in range(2)
                ],
                axis=0,
            )
            both = jnp.concatenate(pieces(q)[:2], axis=0).astype(b16)
            ortho[step, half * 8 * m : (half + 1) * 8 * m, :] = both
            total = total + dot_t(both, both)
        return total

    second = lax.fori_loop(
        0, steps // 8, mix_step, jnp.zeros((8 * m, 8 * m), f32), unroll=2
    )
    second = fold_rows(second, 4 * m)
    col = iota(second.shape, 1)
    second = jnp.where((col // m) % 4 == iota(second.shape, 0) // m, second, 0.0)
    sums = all_reduce(
        fold_rows(second, m) * inv_cells,
        (("gy", gy, py, y2, y2s, y2r), ("gx", gx, px, x2, x2s, x2r)),
    )
    pick_m = where01(iota(sums.shape, 1) % m == iota(sums.shape, 0))
    upper_two, inv_two = factor(dot_t(sums, pick_m, precise))
    tri_out[...] = dot(upper_two, upper_one, precise)

    def pick_two(level):
        row, col = iota((m, 16 * m), 0), iota((m, 16 * m), 1)
        return where01((col % m == row) & ((col // (4 * m)) % 2 < 2 - level))

    col = iota((m, 16 * m), 1)
    last = spread(((inv_two, pick_two),), 2, 8, (col // (8 * m)) * 4 + (col // m) % 4)

    def last_step(step, carry):
        q = fold_rows(dot(last, ortho[step]), 8 * m)
        for g in range(8):
            i = 8 * step + g
            x, f = i // nf, i % nf
            for h in range(halves):
                out[lines(f, x, h, m), :] = q[g * m : (g + 1) * m, h * 128 : (h + 1) * 128]
        return carry

    lax.fori_loop(0, steps // 8, last_step, 0, unroll=2)

    pl.when(gx < px - 1)(send_up.wait_send)
    pl.when(gx > 0)(send_down.wait_send)
    pl.when(gy < py - 1)(send_right.wait_send)
    pl.when(gy > 0)(send_left.wait_send)


def in_tiles(a):
    n, f, x, y = a.shape
    return a.reshape(n, f, x, y // 128, 128).transpose(0, 1, 3, 2, 4).reshape(-1, 128)


def on_device(
    krylov_block, prior_basis, flux_along, flux_across, collision, field_rates,
    wall_table, wall_mask, wall_type,
):
    m, nf, nx, ny = krylov_block.shape
    k, types = prior_basis.shape[0], wall_table.shape[0]
    px, py = lax.axis_size("gx"), lax.axis_size("gy")
    inv_cells = 1.0 / (nf * nx * px * ny * py)
    depth = 6 * m + 2 * (-(-3 * k // 16) * 16)
    steps, width = nf * nx, 8 * m
    rows, halves = nf * m, ny // 128
    hbm = pl.BlockSpec(memory_space=pl.ANY)
    vmem = pl.BlockSpec(memory_space=pltpu.VMEM)
    smem = pl.BlockSpec(memory_space=pltpu.SMEM)
    sems = pltpu.SemaphoreType.DMA
    new, proj, tri = pl.pallas_call(
        functools.partial(kernel, (m, k, nf, nx, ny, types), inv_cells),
        out_shape=(
            jax.ShapeDtypeStruct((halves * m * nf * nx, 128), f32),
            jax.ShapeDtypeStruct((m, k), f32),
            jax.ShapeDtypeStruct((m, m), f32),
        ),
        in_specs=[hbm, hbm, vmem, vmem, vmem, smem, smem, vmem, vmem],
        out_specs=(vmem, vmem, vmem),
        scratch_shapes=[
            pltpu.VMEM((halves * m * nf * nx, 128), f32),
            pltpu.VMEM((halves * k * nf * nx, 128), f32),
            pltpu.VMEM((nx + 4, rows, ny), f32),
            pltpu.VMEM((nx, rows, 128), f32),
            pltpu.VMEM((nx, rows, 128), f32),
            pltpu.VMEM((2, rows, ny), f32),
            pltpu.VMEM((2, rows, ny), f32),
            pltpu.VMEM((nx, rows, ny), f32),
            pltpu.VMEM((2, 2, rows, ny), b16),
            pltpu.VMEM((2, rows, rows), b16),
            pltpu.VMEM((2, rows, rows), b16),
            pltpu.VMEM((steps // 2, depth, ny), b16),
            pltpu.VMEM((steps // 8, 16 * m, ny), b16),
            pltpu.VMEM((m + k, width), f32),
            pltpu.VMEM((py, m + k, width), f32),
            pltpu.VMEM((px, m + k, width), f32),
            pltpu.VMEM((py, m, width), f32),
            pltpu.VMEM((px, m, width), f32),
            sems((2,)), sems((4,)), sems((4,)),
            sems((py - 1,)), sems((py - 1,)), sems((px - 1,)), sems((px - 1,)),
            sems((py - 1,)), sems((py - 1,)), sems((px - 1,)), sems((px - 1,)),
        ],
        compiler_params=pltpu.CompilerParams(
            collective_id=0, has_side_effects=True, vmem_limit_bytes=60 * 1024 * 1024
        ),
    )(
        in_tiles(krylov_block), in_tiles(prior_basis), flux_along, flux_across, collision,
        field_rates, wall_table, wall_mask, wall_type,
    )
    new = new.reshape(m, nf, halves, nx, 128).transpose(0, 1, 3, 2, 4).reshape(m, nf, nx, ny)
    return (new, proj.T, tri)


def solution(mesh):
    placed = (
        P(None, None, "gx", "gy"), P(None, None, "gx", "gy"), P(), P(), P("gx", "gy"),
        P(), P(), P("gx", "gy"), P("gx", "gy"),
    )
    return jax.shard_map(
        on_device,
        mesh=mesh,
        in_specs=placed,
        out_specs=(P(None, None, "gx", "gy"), P(), P()),
        check_vma=False,
    )
```
